256 devices in a mesh: section: 4 (over y), row: 8 (over z_hi, x), col: 8 (over z_lo, core).
Axes of the slice: x: 4, y: 4, z: 8 (z_hi: 2, z_lo: 4; z = z_hi * 4 + z_lo), core: 2. Of those that a mesh axis runs over, the one named last changes fastest.
Arguments:
- section_inputs: bfloat16 [4, 2048, 2048], P('section', 'col', 'row'), may hold values from -6 to 6
- out_grad: bfloat16 [4, 2048, 2048], P('section', 'col', 'row'), may hold values from -6 to 6
- saved_gate: bfloat16 [4, 2048, 8192], P('section', 'row', 'col'), may hold values from -6 to 6
- saved_up: bfloat16 [4, 2048, 8192], P('section', 'row', 'col'), may hold values from -6 to 6
- gate_weight: bfloat16 [4, 2048, 8192], P('section', 'row', 'col'), may hold values from -0.125 to 0.125
- up_weight: bfloat16 [4, 2048, 8192], P('section', 'row', 'col'), may hold values from -0.125 to 0.125
- down_weight: bfloat16 [4, 8192, 2048], P('section', 'col', 'row'), may hold values from -0.0625 to 0.0625
- momentum_gate: float32 [4, 2048, 8192], P('section', 'row', 'col'), may hold values from -6 to 6
- momentum_up: float32 [4, 2048, 8192], P('section', 'row', 'col'), may hold values from -6 to 6
- momentum_down: float32 [4, 8192, 2048], P('section', 'col', 'row'), may hold values from -6 to 6
- noise_gate: bfloat16 [4, 2048, 8192], P('section', 'row', 'col'), may hold values from -6 to 6
- noise_up: bfloat16 [4, 2048, 8192], P('section', 'row', 'col'), may hold values from -6 to 6
- noise_down: bfloat16 [4, 8192, 2048], P('section', 'col', 'row'), may hold values from -6 to 6
Outputs:
- prev_grads: bfloat16 [4, 2048, 2048], P('section', 'col', 'row')
- new_gate: bfloat16 [4, 2048, 8192], P('section', 'row', 'col')
- new_up: bfloat16 [4, 2048, 8192], P('section', 'row', 'col')
- new_down: bfloat16 [4, 8192, 2048], P('section', 'col', 'row')
- next_momentum_gate: float32 [4, 2048, 8192], P('section', 'row', 'col')
- next_momentum_up: float32 [4, 2048, 8192], P('section', 'row', 'col')
- next_momentum_down: float32 [4, 8192, 2048], P('section', 'col', 'row')
The draws below stay inside these ranges and needn't reach their ends.
All inputs are finite; a program needn't handle non-finite values.
Results may differ from the reference program's by a relative error of at most 0.025.
Values may be sent and summed in bfloat16 or wider, within the bound.
A program may use at most 128 MiB of HBM per device.

```python
import jax
import jax.numpy as jnp
from jax import lax

D = 2048
FF = 8192
SECTIONS = 4
TOKENS = 2048
N_ROW = 8
N_COL = 8


def block_levels(stream_key, shape, split, smallest, high):
    loudness = 1.0
    for axis_at, parts in split:
        steps = jax.random.uniform(jax.random.fold_in(jax.random.fold_in(stream_key, 6), axis_at), (parts,), jnp.float32, smallest / len(split), high / len(split))
        loudness = loudness * jnp.repeat(jnp.exp(steps), shape[axis_at] // parts).reshape((-1,) + (1,) * (len(shape) - 1 - axis_at))
    return loudness


def centred(key, extent, scale, limit, shards=(), held_as=jnp.bfloat16):
    drawn = scale * jax.random.normal(key, extent, jnp.float32)
    if shards:
        drawn = drawn * block_levels(key, extent, shards, -0.22, 0.18)
    return jnp.clip(drawn, -limit, limit).astype(held_as)


def setup_inputs(seed: int = 0) -> dict:
    splits = jax.random.split(jax.random.key(seed), 14)
    section_inputs = centred(splits[0], (SECTIONS, TOKENS, D), 1.0, 6.0, ((0, 4), (1, 8), (2, 8)))
    out_grad = centred(splits[1], (SECTIONS, TOKENS, D), 1.0, 6.0, ((0, 4), (1, 8), (2, 8)))
    saved_gate = centred(splits[2], (SECTIONS, TOKENS, FF), 1.0, 6.0, ((0, 4), (1, 8), (2, 8)))
    saved_up = centred(splits[3], (SECTIONS, TOKENS, FF), 1.0, 6.0, ((0, 4), (1, 8), (2, 8)))
    gate_weight = centred(splits[4], (SECTIONS, D, FF), D ** -0.5, 0.125, ((0, 4), (1, 8), (2, 8)))
    up_weight = centred(splits[5], (SECTIONS, D, FF), D ** -0.5, 0.125, ((0, 4), (1, 8), (2, 8)))
    down_weight = centred(splits[6], (SECTIONS, FF, D), FF ** -0.5, 0.0625, ((0, 4), (1, 8), (2, 8)))
    momentum_gate = centred(splits[7], (SECTIONS, D, FF), 1.0, 6.0, ((0, 4), (1, 8), (2, 8)), jnp.float32)
    momentum_up = centred(splits[8], (SECTIONS, D, FF), 1.0, 6.0, ((0, 4), (1, 8), (2, 8)), jnp.float32)
    momentum_down = centred(splits[9], (SECTIONS, FF, D), 1.0, 6.0, ((0, 4), (1, 8), (2, 8)), jnp.float32)
    noise_gate = centred(splits[10], (SECTIONS, D, FF), 1.0, 6.0, ((0, 4), (1, 8), (2, 8)))
    noise_up = centred(splits[11], (SECTIONS, D, FF), 1.0, 6.0, ((0, 4), (1, 8), (2, 8)))
    noise_down = centred(splits[12], (SECTIONS, FF, D), 1.0, 6.0, ((0, 4), (1, 8), (2, 8)))
    return dict(section_inputs=section_inputs, out_grad=out_grad, saved_gate=saved_gate, saved_up=saved_up, gate_weight=gate_weight, up_weight=up_weight, down_weight=down_weight, momentum_gate=momentum_gate, momentum_up=momentum_up, momentum_down=momentum_down, noise_gate=noise_gate, noise_up=noise_up, noise_down=noise_down)


FRICTION = 0.1
DRIFT = 0.01


def blockwise_sum(pairs, blocks):
    width = pairs[0][0].shape[1] // blocks
    total = jnp.zeros((pairs[0][0].shape[0], pairs[0][1].shape[1]), jnp.float32)
    for block in range(blocks):
        partial_value = jnp.zeros_like(total)
        for left, right in pairs:
            left_block = left[:, block * width:(block + 1) * width]
            right_block = right[block * width:(block + 1) * width, :]
            partial_value = partial_value + jnp.dot(left_block, right_block, preferred_element_type=jnp.float32)
        rounded = lax.optimization_barrier(partial_value.astype(jnp.bfloat16))
        total = total + rounded.astype(jnp.float32)
    return total


def pre_grads(hidden_grad, gate_pre, up_pre):
    gate_wide = gate_pre.astype(jnp.float32)
    up_wide = up_pre.astype(jnp.float32)
    sigmoid_gate = jax.nn.sigmoid(gate_wide)
    silu_gate = gate_wide * sigmoid_gate
    slope = sigmoid_gate * (1.0 + gate_wide * (1.0 - sigmoid_gate))
    gate_grad = (hidden_grad * up_wide * slope).astype(jnp.bfloat16)
    up_grad = (hidden_grad * silu_gate).astype(jnp.bfloat16)
    hidden_saved = (silu_gate * up_wide).astype(jnp.bfloat16)
    return hidden_saved, gate_grad, up_grad


def sghmc_step(weight, momentum, gradient, noise, kick_scale):
    moved = (1.0 - FRICTION) * momentum - kick_scale * gradient + (2.0 * FRICTION) ** 0.5 * noise.astype(jnp.float32)
    fresh = (weight.astype(jnp.float32) + DRIFT * moved).astype(jnp.bfloat16)
    return fresh, moved


def reference(section_inputs, out_grad, saved_gate, saved_up, gate_weight, up_weight, down_weight, momentum_gate, momentum_up, momentum_down, noise_gate, noise_up, noise_down):
    kick_scale = float(TOKENS) ** -0.5
    input_grads = []
    gates, ups, downs, gate_moms, up_moms, down_moms = [], [], [], [], [], []
    for section in range(SECTIONS):
        inputs_now = section_inputs[section]
        grads_now = out_grad[section]
        hidden_grad = blockwise_sum([(grads_now, down_weight[section].T)], N_ROW)
        hidden_saved, gate_grad, up_grad = pre_grads(hidden_grad, saved_gate[section], saved_up[section])
        down_wgrad = jnp.dot(hidden_saved.T, grads_now, preferred_element_type=jnp.float32)
        gate_wgrad = jnp.dot(inputs_now.T, gate_grad, preferred_element_type=jnp.float32)
        up_wgrad = jnp.dot(inputs_now.T, up_grad, preferred_element_type=jnp.float32)
        input_grad = blockwise_sum([(gate_grad, gate_weight[section].T), (up_grad, up_weight[section].T)], N_COL).astype(jnp.bfloat16)
        input_grads.append(input_grad)
        fresh, moved = sghmc_step(gate_weight[section], momentum_gate[section], gate_wgrad, noise_gate[section], kick_scale)
        gates.append(fresh)
        gate_moms.append(moved)
        fresh, moved = sghmc_step(up_weight[section], momentum_up[section], up_wgrad, noise_up[section], kick_scale)
        ups.append(fresh)
        up_moms.append(moved)
        fresh, moved = sghmc_step(down_weight[section], momentum_down[section], down_wgrad, noise_down[section], kick_scale)
        downs.append(fresh)
        down_moms.append(moved)
    stacked = jnp.stack(input_grads)
    prev_grads = jnp.concatenate([stacked[1:], jnp.zeros_like(stacked[:1])], axis=0)
    return (prev_grads, jnp.stack(gates), jnp.stack(ups), jnp.stack(downs), jnp.stack(gate_moms), jnp.stack(up_moms), jnp.stack(down_moms))
```

```python
import functools

import jax
import jax.numpy as jnp
from jax import lax
from jax.experimental import pallas as pl
from jax.experimental.pallas import tpu as pltpu
from jax.sharding import PartitionSpec as P

FRICTION = 0.1
DRIFT = 0.01
MESH = pl.DeviceIdType.MESH
BF = jnp.bfloat16
F32 = jnp.float32
NC = 4

DN, SGX, SUX, GTX, UPX = 0, NC, 2 * NC, 3 * NC, 4 * NC
DYR = 5 * NC
DYC = DYR + 8
XR = DYC + 8
XC = XR + 8
RS = XC + 8
AG = RS + 3 * NC
AF = AG + 6 * NC
WX = AF + 6 * NC
DXC = WX + 3 * NC
DXR = DXC + 4
FIN = DXR + 8
NSEM = FIN + 1


def nt(a, b):
    return lax.dot_general(a, b, (((1,), (1,)), ((), ())), preferred_element_type=F32)


def nn(a, b):
    return jnp.dot(a, b, preferred_element_type=F32)


def kernel(
    kick,
    x_in, dy_in, sg_in, su_in, wg_in, wu_in, wd_in, mg_in, mu_in, md_in, ng_in, nu_in, nd_in,
    prev_out, wg_out, wu_out, wd_out, mg_out, mu_out, md_out,
    x_stage, dyf, xt, down_f, gate_f, up_f, sg_f, su_f, hgs, rsr, ht, g, u,
    wds, wgs, wus, wdr, wgr, wur, mg, mu, md, ng, nu, nd, wg, wu, wd,
    acc, dxs, dxr, psend, precv, fin, finr, outv,
    ssem, rsem, lsem, osem,
):
    tb, fb = x_in.shape[1], x_in.shape[2]
    half = sg_in.shape[2] // 2
    cw = half // NC
    xb = 2 * tb

    y, row, col = lax.axis_index("section"), lax.axis_index("row"), lax.axis_index("col")
    zh, x, zl, core = row // 4, row % 4, col // 2, col % 2
    z = zh * 4 + zl
    oh = 1 - zh

    def at_z(zz):
        return (y, (zz // 4) * 4 + x, (zz % 4) * 2 + core)

    def at_x(xx):
        return (y, zh * 4 + xx, col)

    partner = (y, oh * 4 + x, col)
    z_next, z_prev = at_z((z + 1) % 8), at_z((z + 7) % 8)
    x1, x2, x3 = (x + 1) % 4, (x + 2) % 4, (x + 3) % 4
    x_next, x_prev, x_far = at_x(x1), at_x(x3), at_x(x2)
    twin = (y, row, zl * 2 + 1 - core)
    y_prev, y_next = ((y + 3) % 4, row, col), ((y + 1) % 4, row, col)

    def rcopy(src, dst, sem, to):
        return pltpu.make_async_remote_copy(
            src_ref=src, dst_ref=dst, send_sem=ssem.at[sem], recv_sem=rsem.at[sem],
            device_id=to, device_id_type=MESH,
        )

    def send(src, dst, sem, to):
        rcopy(src, dst, sem, to).start()

    def got(dst, sem):
        rcopy(dst, dst, sem, partner).wait_recv()

    def sent(src, sem):
        rcopy(src, src, sem, partner).wait_send()

    def cols(at, j):
        return pl.ds(pl.multiple_of(at * half + j * cw, cw), cw)

    def chunk(j):
        return pl.ds(pl.multiple_of(j * cw, cw), cw)

    def place(zz, kk):
        return ((((zz % 2) * 2 + kk) * 2) + (zz % 4) // 2) * tb

    def dy_slot(zz, kk, first=0, size=tb):
        return dyf.at[zz // 4, pl.ds(pl.multiple_of(place(zz, kk) + first, 16), size)]

    def x_slot(zz, kk, first=0, size=fb):
        return xt.at[zz // 4, pl.ds(first, size), pl.ds(pl.multiple_of(place(zz, kk), tb), tb)]

    bar = pltpu.get_barrier_semaphore()
    for to in (partner, z_next, z_prev, x_next, x_prev, x_far, twin, y_next):
        pl.semaphore_signal(bar, inc=1, device_id=to, device_id_type=MESH)

    own_half = pl.ds(pl.multiple_of(zh * half, half), half)
    loads = [
        pltpu.make_async_copy(s, d, lsem.at[i])
        for i, (s, d) in enumerate([
            (x_in.at[0], x_stage),
            (dy_in.at[0], dy_slot(z, core)),
            (wd_in.at[0, own_half], down_f.at[zh]),
            (sg_in.at[0, :, own_half], sg_f.at[zh]),
            (su_in.at[0, :, own_half], su_f.at[zh]),
            (wg_in.at[0, :, own_half], gate_f.at[zh]),
            (wu_in.at[0, :, own_half], up_f.at[zh]),
            (mg_in.at[0], mg), (mu_in.at[0], mu), (md_in.at[0], md),
            (ng_in.at[0], ng), (nu_in.at[0], nu), (nd_in.at[0], nd),
            (wg_in.at[0], wg), (wu_in.at[0], wu), (wd_in.at[0], wd),
        ])
    ]
    for load in loads:
        load.start()
    pl.semaphore_wait(bar, 8)

    def ring(slot, base, cbase, step):
        size = tb if slot is dy_slot else fb
        back, ahead = (z + 8 - step) % 8, (z + step) % 8
        if step < 3:
            send(slot(back, core), slot(back, core), base + 2 * step, z_next)
            send(slot(ahead, core), slot(ahead, core), base + 2 * step + 1, z_prev)
        elif step == 3:
            lo, hi = (0, size // 2), (size // 2, size // 2)
            send(slot(back, core, *lo), slot(back, core, *lo), base + 6, z_next)
            send(slot(ahead, core, *hi), slot(ahead, core, *hi), base + 7, z_prev)
        if step == 0 or step == 4:
            send(slot(back, core), slot(back, core), cbase + 2 * step - (step == 4), twin)
        else:
            send(slot(back, core), slot(back, core), cbase + 2 * step - 1, twin)
            send(slot(ahead, core), slot(ahead, core), cbase + 2 * step, twin)

    def ring_got(slot, base, step):
        size = tb if slot is dy_slot else fb
        back, ahead = (z + 8 - step) % 8, (z + step) % 8
        if step < 4:
            got(slot(back, core), base + 2 * step - 2)
            got(slot(ahead, core), base + 2 * step - 1)
        else:
            got(slot(back, core, 0, size // 2), base + 6)
            got(slot(ahead, core, size // 2, size // 2), base + 7)

    def ring_order():
        return [(0, z)] + [
            (2 * s - 1 + d, (z + 8 - s) % 8 if d == 0 else (z + s) % 8) for s in (1, 2, 3) for d in (0, 1)
        ] + [(7, (z + 4) % 8)]

    def ring_sent(slot, base, cbase):
        size = tb if slot is dy_slot else fb
        for step in range(3):
            sent(slot(z, core), base + 2 * step)
            sent(slot(z, core), base + 2 * step + 1)
        sent(slot(z, core, 0, size // 2), base + 6)
        sent(slot(z, core, 0, size // 2), base + 7)
        for i in range(8):
            sent(slot(z, core), cbase + i)

    loads[1].wait()
    ring(dy_slot, DYR, DYC, 0)

    @pl.loop(0, NC)
    def _(j):
        there = pl.ds(pl.multiple_of(oh * half + j * cw, cw), cw)
        send(wd_in.at[0, there], down_f.at[zh, chunk(j)], DN + j, partner)

    loads[0].wait()
    x_slot_own = x_slot(z, core)
    x_slot_own[...] = x_stage[...].astype(F32).T.astype(BF)
    acc[...] = jnp.zeros_like(acc)

    for step in (1, 2, 3):
        ring_got(dy_slot, DYR, step)
        ring(dy_slot, DYR, DYC, step)

    @pl.loop(0, NC)
    def _(j):
        send(sg_in.at[0, :, cols(oh, j)], sg_f.at[zh, :, chunk(j)], SGX + j, partner)
        send(su_in.at[0, :, cols(oh, j)], su_f.at[zh, :, chunk(j)], SUX + j, partner)

    ring_got(dy_slot, DYR, 4)
    ring(dy_slot, DYR, DYC, 4)
    loads[2].wait()
    for i, zz in ring_order():
        got(dy_slot(zz, 1 - core), DYC + i)

    def partial_hidden(j):
        got(down_f.at[oh, chunk(j)], DN + j)

        @pl.loop(0, 4)
        def _(xx):
            rows = pl.ds(pl.multiple_of(xx * xb, xb), xb)
            hgs[j, xx] = (
                nt(dyf[0, rows, :], down_f[0, chunk(j), :]) + nt(dyf[1, rows, :], down_f[1, chunk(j), :])
            ).astype(BF)

        send(hgs.at[j, x1], rsr.at[j, 0], RS + 3 * j, x_next)
        send(hgs.at[j, x2], rsr.at[j, 1], RS + 3 * j + 1, x_far)
        send(hgs.at[j, x3], rsr.at[j, 2], RS + 3 * j + 2, x_prev)

    ring(x_slot, XR, XC, 0)
    pl.loop(0, NC)(partial_hidden)

    @pl.loop(0, NC)
    def _(j):
        send(wg_in.at[0, :, cols(oh, j)], gate_f.at[zh, :, chunk(j)], GTX + j, partner)
        send(wu_in.at[0, :, cols(oh, j)], up_f.at[zh, :, chunk(j)], UPX + j, partner)

    for step in (1, 2, 3):
        ring_got(x_slot, XR, step)
        ring(x_slot, XR, XC, step)
    for i in (3, 4, 5, 6):
        loads[i].wait()

    def activations(j):
        for d in range(3):
            got(rsr.at[j, d], RS + 3 * j + d)
        got(sg_f.at[oh, :, chunk(j)], SGX + j)
        got(su_f.at[oh, :, chunk(j)], SUX + j)
        for part in range(2):
            rows = pl.ds(part * tb, tb)
            hidden_grad = hgs[j, x, rows, :].astype(F32)
            for d in range(3):
                hidden_grad = hidden_grad + rsr[j, d, rows, :].astype(F32)
            gate_pre = sg_f[part, :, chunk(j)].astype(F32)
            up_pre = su_f[part, :, chunk(j)].astype(F32)
            sigmoid_gate = jax.nn.sigmoid(gate_pre)
            silu_gate = gate_pre * sigmoid_gate
            slope = sigmoid_gate * (1.0 + gate_pre * (1.0 - sigmoid_gate))
            g[j, x, rows, :] = (hidden_grad * up_pre * slope).astype(BF)
            u[j, x, rows, :] = (hidden_grad * silu_gate).astype(BF)
            ht[j, x, :, rows] = (silu_gate * up_pre).T.astype(BF)
        for i, ref in enumerate((ht, g, u)):
            send(ref.at[j, x], ref.at[j, x], AG + 6 * j + i, x_next)
            send(ref.at[j, x], ref.at[j, x], AG + 6 * j + 3 + i, x_prev)

    def halves(ref, j, xx, second):
        size = ref.shape[2] // 2
        return ref.at[j, xx, pl.ds(second * size, size)]

    def forward(j):
        for i, ref in enumerate((ht, g, u)):
            got(ref.at[j, x3], AG + 6 * j + i)
            send(halves(ref, j, x3, 0), halves(ref, j, x3, 0), AF + 6 * j + i, x_next)
            got(ref.at[j, x1], AG + 6 * j + 3 + i)
            send(halves(ref, j, x1, 1), halves(ref, j, x1, 1), AF + 6 * j + 3 + i, x_prev)

    def step_columns(i, w, m, n, w_out, m_out, at, j, grad):
        c = cols(at, j)
        moved = (1.0 - FRICTION) * m[:, c] - kick * grad + (2.0 * FRICTION) ** 0.5 * n[:, c].astype(F32)
        m[:, c] = moved
        w[:, c] = (w[:, c].astype(F32) + DRIFT * moved).astype(BF)
        pltpu.make_async_copy(m.at[:, c], m_out.at[0, :, c], osem.at[at, j, 2 * i]).start()
        pltpu.make_async_copy(w.at[:, c], w_out.at[0, :, c], osem.at[at, j, 2 * i + 1]).start()

    def step_rows(at, j, grad):
        c = cols(at, j)
        moved = (1.0 - FRICTION) * md[c, :] - kick * grad + (2.0 * FRICTION) ** 0.5 * nd[c, :].astype(F32)
        md[c, :] = moved
        wd[c, :] = (wd[c, :].astype(F32) + DRIFT * moved).astype(BF)
        pltpu.make_async_copy(md.at[c, :], md_out.at[0, c, :], osem.at[at, j, 4]).start()
        pltpu.make_async_copy(wd.at[c, :], wd_out.at[0, c, :], osem.at[at, j, 5]).start()

    def weight_grads(j):
        for i, ref in enumerate((ht, g, u)):
            got(halves(ref, j, x2, 0), AF + 6 * j + i)
            got(halves(ref, j, x2, 1), AF + 6 * j + 3 + i)

        def down_grad(at):
            total = nn(ht[j, 0], dyf[at, pl.ds(0, xb), :])
            for xx in range(1, 4):
                total = total + nn(ht[j, xx], dyf[at, pl.ds(xx * xb, xb), :])
            return total

        def column_grad(at, ref):
            total = nn(xt[at, :, pl.ds(0, xb)], ref[j, 0])
            for xx in range(1, 4):
                total = total + nn(xt[at, :, pl.ds(xx * xb, xb)], ref[j, xx])
            return total

        wds[j] = down_grad(oh).astype(BF)
        send(wds.at[j], wdr.at[j], WX + 3 * j, partner)
        wgs[j] = column_grad(oh, g).astype(BF)
        send(wgs.at[j], wgr.at[j], WX + 3 * j + 1, partner)
        wus[j] = column_grad(oh, u).astype(BF)
        send(wus.at[j], wur.at[j], WX + 3 * j + 2, partner)

        got(gate_f.at[oh, :, chunk(j)], GTX + j)
        got(up_f.at[oh, :, chunk(j)], UPX + j)

        @pl.loop(0, 4)
        def _(xx):
            rows = pl.ds(pl.multiple_of(xx * xb, xb), xb)
            for at in range(2):
                acc[at, rows, :] += nt(g[j, xx], gate_f[at, :, chunk(j)]) + nt(u[j, xx], up_f[at, :, chunk(j)])

        step_rows(zh, j, down_grad(zh))
        step_columns(0, wg, mg, ng, wg_out, mg_out, zh, j, column_grad(zh, g))
        step_columns(1, wu, mu, nu, wu_out, mu_out, zh, j, column_grad(zh, u))

    def partner_grads(j):
        got(wdr.at[j], WX + 3 * j)
        step_rows(oh, j, wdr[j].astype(F32))
        got(wgr.at[j], WX + 3 * j + 1)
        step_columns(0, wg, mg, ng, wg_out, mg_out, oh, j, wgr[j].astype(F32))
        got(wur.at[j], WX + 3 * j + 2)
        step_columns(1, wu, mu, nu, wu_out, mu_out, oh, j, wur[j].astype(F32))

    activations(0)
    ring_got(x_slot, XR, 4)
    ring(x_slot, XR, XC, 4)
    for i, zz in ring_order():
        got(x_slot(zz, 1 - core), XC + i)
    for i in range(7, 16):
        loads[i].wait()

    @pl.loop(1, NC + 2)
    def _(i):
        @pl.when(i < NC)
        def _():
            activations(i)

        @pl.when(i <= NC)
        def _():
            forward(i - 1)

        @pl.when(i >= 2)
        def _():
            weight_grads(i - 2)

    for m in range(2):
        for at in range(2):
            rows = pl.ds(pl.multiple_of((1 - core + 2 * m) * xb, xb), xb)
            dxs[at, m] = acc[at, rows, :].astype(BF)
            send(dxs.at[at, m], dxr.at[at, m], DXC + 2 * m + at, twin)
    for m in range(2):
        for at in range(2):
            got(dxr.at[at, m], DXC + 2 * m + at)

    def part(zz, first=0, size=tb):
        at, late, m = zz // 4, (zz % 4) // 2, zz % 2
        mine = pl.ds(pl.multiple_of(((core + 2 * m) * 2 + late) * tb + first, 16), size)
        other = pl.ds(pl.multiple_of(late * tb + first, 16), size)
        return acc[at, mine, :] + dxr[at, m, other, :].astype(F32)

    ht2 = tb // 2
    far = (z + 4) % 8
    psend[0, 0, pl.ds(0, ht2), :] = part(far, 0, ht2).astype(BF)
    send(psend.at[0, 0, pl.ds(0, ht2)], precv.at[0, 0, pl.ds(0, ht2)], DXR, z_next)
    psend[1, 0, pl.ds(0, ht2), :] = part(far, ht2, ht2).astype(BF)
    send(psend.at[1, 0, pl.ds(0, ht2)], precv.at[1, 0, pl.ds(0, ht2)], DXR + 1, z_prev)
    for step in (1, 2, 3):
        for d in range(2):
            to = (z + 4 - step) % 8 if d == 0 else (z + 4 + step) % 8
            if step == 1:
                got(precv.at[d, 0, pl.ds(0, ht2)], DXR + d)
                psend[d, 1, pl.ds((1 - d) * ht2, ht2), :] = part(to, (1 - d) * ht2, ht2).astype(BF)
                psend[d, 1, pl.ds(d * ht2, ht2), :] = (
                    part(to, d * ht2, ht2) + precv[d, 0, pl.ds(0, ht2), :].astype(F32)
                ).astype(BF)
            else:
                got(precv.at[d, step - 1], DXR + 2 * (step - 1) + d)
                psend[d, step] = (part(to) + precv[d, step - 1].astype(F32)).astype(BF)
            send(psend.at[d, step], precv.at[d, step], DXR + 2 * step + d, z_next if d == 0 else z_prev)

    pl.loop(0, NC)(partner_grads)

    got(precv.at[0, 3], DXR + 6)
    got(precv.at[1, 3], DXR + 7)
    fin[...] = (part(z) + precv[0, 3].astype(F32) + precv[1, 3].astype(F32)).astype(BF)
    send(fin, finr, FIN, y_prev)
    got(finr, FIN)
    outv[...] = jnp.where(y == 3, jnp.zeros_like(finr), finr[...])
    last = pltpu.make_async_copy(outv, prev_out.at[0], lsem.at[0])
    last.start()

    ring_sent(dy_slot, DYR, DYC)
    ring_sent(x_slot, XR, XC)

    @pl.loop(0, NC)
    def _(j):
        sent(down_f.at[0, chunk(j)], DN + j)
        for ref, base in ((sg_f, SGX), (su_f, SUX), (gate_f, GTX), (up_f, UPX)):
            sent(ref.at[0, :, chunk(j)], base + j)
        for d in range(3):
            sent(rsr.at[j, d], RS + 3 * j + d)
        for i, ref in enumerate((ht, g, u)):
            for d in range(2):
                sent(ref.at[j, 0], AG + 6 * j + 3 * d + i)
                sent(halves(ref, j, 0, 0), AF + 6 * j + 3 * d + i)
        for i, ref in enumerate((wds, wgs, wus)):
            sent(ref.at[j], WX + 3 * j + i)
        for at in range(2):
            c = cols(at, j)
            for i, (w, m, w_out, m_out) in enumerate(((wg, mg, wg_out, mg_out), (wu, mu, wu_out, mu_out))):
                pltpu.make_async_copy(m.at[:, c], m_out.at[0, :, c], osem.at[at, j, 2 * i]).wait()
                pltpu.make_async_copy(w.at[:, c], w_out.at[0, :, c], osem.at[at, j, 2 * i + 1]).wait()
            pltpu.make_async_copy(md.at[c, :], md_out.at[0, c, :], osem.at[at, j, 4]).wait()
            pltpu.make_async_copy(wd.at[c, :], wd_out.at[0, c, :], osem.at[at, j, 5]).wait()

    for i in range(4):
        sent(dxs.at[0, 0], DXC + i)
    for d in range(2):
        sent(psend.at[d, 0, pl.ds(0, ht2)], DXR + d)
        for step in (1, 2, 3):
            sent(psend.at[d, step], DXR + 2 * step + d)
    sent(fin, FIN)
    last.wait()


def shards(*args):
    x_in, sg_in, wd_in = args[0], args[2], args[6]
    tb, fb = x_in.shape[1], x_in.shape[2]
    hb = sg_in.shape[2]
    half = hb // 2
    cw = half // NC
    tokens = tb * lax.axis_size("row")
    kick = float(tokens) ** (-0.5)
    v = pltpu.VMEM
    scratch = [
        v((tb, fb), BF),
        v((2, tokens, fb), BF),
        v((2, fb, tokens), BF),
        v((2, half, fb), BF),
        v((2, fb, half), BF),
        v((2, fb, half), BF),
        v((2, tb, half), BF),
        v((2, tb, half), BF),
        v((NC, 4, 2 * tb, cw), BF),
        v((NC, 3, 2 * tb, cw), BF),
        v((NC, 4, cw, 2 * tb), BF),
        v((NC, 4, 2 * tb, cw), BF),
        v((NC, 4, 2 * tb, cw), BF),
        v((NC, cw, fb), BF), v((NC, fb, cw), BF), v((NC, fb, cw), BF),
        v((NC, cw, fb), BF), v((NC, fb, cw), BF), v((NC, fb, cw), BF),
        v((fb, hb), F32), v((fb, hb), F32), v((hb, fb), F32),
        v((fb, hb), BF), v((fb, hb), BF), v((hb, fb), BF),
        v((fb, hb), BF), v((fb, hb), BF), v((hb, fb), BF),
        v((2, tokens, fb), F32),
        v((2, 2, 2 * tb, fb), BF),
        v((2, 2, 2 * tb, fb), BF),
        v((2, 4, tb, fb), BF),
        v((2, 4, tb, fb), BF),
        v((tb, fb), BF), v((tb, fb), BF), v((tb, fb), BF),
        pltpu.SemaphoreType.DMA((NSEM,)),
        pltpu.SemaphoreType.DMA((NSEM,)),
        pltpu.SemaphoreType.DMA((16,)),
        pltpu.SemaphoreType.DMA((2, NC, 6)),
    ]
    shape = jax.ShapeDtypeStruct
    outs = (
        shape(args[0].shape, BF),
        shape(args[4].shape, BF), shape(args[5].shape, BF), shape(args[6].shape, BF),
        shape(args[7].shape, F32), shape(args[8].shape, F32), shape(args[9].shape, F32),
    )
    work = 12 * tokens * fb * hb
    return pl.pallas_call(
        functools.partial(kernel, kick),
        out_shape=outs,
        in_specs=[pl.BlockSpec(memory_space=pl.ANY)] * 13,
        out_specs=[pl.BlockSpec(memory_space=pl.ANY)] * 7,
        scratch_shapes=scratch,
        compiler_params=pltpu.CompilerParams(
            collective_id=1, has_side_effects=True, vmem_limit_bytes=56 << 20
        ),
        cost_estimate=pl.CostEstimate(flops=work, bytes_accessed=12 << 20, transcendentals=0),
        name="relayed_step",
    )(*args)


def solution(mesh):
    feature = P("section", "col", "row")
    hidden = P("section", "row", "col")
    in_specs = (
        feature, feature, hidden, hidden, hidden, hidden, feature,
        hidden, hidden, feature, hidden, hidden, feature,
    )
    out_specs = (feature, hidden, hidden, feature, hidden, hidden, feature)
    return jax.shard_map(shards, mesh=mesh, in_specs=in_specs, out_specs=out_specs, check_vma=False)
```

```python
import functools

import jax
import jax.numpy as jnp
from jax import lax
from jax.experimental import pallas as pl
from jax.experimental.pallas import tpu as pltpu
from jax.sharding import PartitionSpec as P

FRICTION = 0.1
DRIFT = 0.01
MESH = pl.DeviceIdType.MESH
BF = jnp.bfloat16
F32 = jnp.float32
NC = 4
DN_FIRST = 4
SG_FIRST = 4
HG_FIRST = 2
X_FIRST = True
X_BESIDE = {1: (), 2: (), 3: (0,), 4: ()}
LAG = 3
X_AFTER = ()
X_TURNS = ((1, 0), (2, 1), (3, 2), (4, 3))

DN, SGX, SUX, GTX, UPX = 0, NC, 2 * NC, 3 * NC, 4 * NC
DYR = 5 * NC
DYC = DYR + 14
XR = DYC + 8
XC = XR + 14
RS = XC + 8
AG = RS + 3 * NC
AF = AG + 4 * NC
WX = AF + 4 * NC
HA = WX + 3 * NC
HF = HA + 2 * NC
DXC = HF + 2 * NC
DXR = DXC + 4
FIN = DXR + 16
NSEM = FIN + 2


def nt(a, b):
    return lax.dot_general(a, b, (((1,), (1,)), ((), ())), preferred_element_type=F32)


def nn(a, b):
    return jnp.dot(a, b, preferred_element_type=F32)


def kernel(
    x_in, dy_in, sg_in, su_in, wg_in, wu_in, wd_in,
    prev_out, gg_out, gu_out, gd_out,
    x_stage, dyf, xt, down_f, gate_f, up_f, sg_f, su_f, hgs, rsr, ht, g, u,
    wds, wgs, wus, owd, owg, owu, acc, dxs, dxr, psend, precv, fin,
    ssem, rsem, lsem, osem,
):
    tb, fb = x_in.shape[1], x_in.shape[2]
    half = sg_in.shape[2] // 2
    cw = half // NC
    xb = 2 * tb

    y, row, col = lax.axis_index("section"), lax.axis_index("row"), lax.axis_index("col")
    zh, x, zl, core = row // 4, row % 4, col // 2, col % 2
    z = zh * 4 + zl
    oh = 1 - zh

    def at_z(zz):
        return (y, (zz // 4) * 4 + x, (zz % 4) * 2 + core)

    def at_x(xx):
        return (y, zh * 4 + xx, col)

    partner = (y, oh * 4 + x, col)
    z_next, z_prev = at_z((z + 1) % 8), at_z((z + 7) % 8)
    x1, x2, x3 = (x + 1) % 4, (x + 2) % 4, (x + 3) % 4
    x_next, x_prev, x_far = at_x(x1), at_x(x3), at_x(x2)
    twin = (y, row, zl * 2 + 1 - core)
    y_prev, y_next = ((y + 3) % 4, row, col), ((y + 1) % 4, row, col)

    def rcopy(src, dst, sem, to):
        return pltpu.make_async_remote_copy(
            src_ref=src, dst_ref=dst, send_sem=ssem.at[sem], recv_sem=rsem.at[sem],
            device_id=to, device_id_type=MESH,
        )

    def send(src, dst, sem, to):
        rcopy(src, dst, sem, to).start()

    def got(dst, sem):
        rcopy(dst, dst, sem, partner).wait_recv()

    def sent(src, sem):
        rcopy(src, src, sem, partner).wait_send()

    def cols(at, j):
        return pl.ds(pl.multiple_of(at * half + j * cw, cw), cw)

    def chunk(j):
        return pl.ds(pl.multiple_of(j * cw, cw), cw)

    def place(zz, kk):
        return ((((zz % 2) * 2 + kk) * 2) + (zz % 4) // 2) * tb

    def dy_slot(zz, kk, first=0, size=tb):
        return dyf.at[zz // 4, pl.ds(pl.multiple_of(place(zz, kk) + first, 16), size)]

    def x_slot(zz, kk, first=0, size=fb):
        return xt.at[zz // 4, pl.ds(first, size), pl.ds(pl.multiple_of(place(zz, kk), tb), tb)]

    bar = pltpu.get_barrier_semaphore()
    for to in (partner, z_next, z_prev, x_next, x_prev, x_far, twin, y_next):
        pl.semaphore_signal(bar, inc=1, device_id=to, device_id_type=MESH)

    own_half = pl.ds(pl.multiple_of(zh * half, half), half)
    loads = [
        pltpu.make_async_copy(s, d, lsem.at[i])
        for i, (s, d) in enumerate([
            (x_in.at[0], x_stage),
            (dy_in.at[0], dy_slot(z, core)),
            (wd_in.at[0, own_half], down_f.at[zh]),
            (sg_in.at[0, :, own_half], sg_f.at[zh]),
            (su_in.at[0, :, own_half], su_f.at[zh]),
            (wg_in.at[0, :, own_half], gate_f.at[zh]),
            (wu_in.at[0, :, own_half], up_f.at[zh]),
        ])
    ]
    for load in loads:
        load.start()
    pl.semaphore_wait(bar, 8)

    def pieces(slot):
        size = (tb if slot is dy_slot else fb) // 2
        return (0, size), (size, size)

    def ring_sem(base, step, d, p):
        return base + (4 * step + 2 * d + p if step < 3 else 12 + d)

    def ring(slot, base, cbase, step):
        back, ahead = (z + 8 - step) % 8, (z + step) % 8
        for p, cut in enumerate(pieces(slot)):
            for d, (block, to) in enumerate(((back, z_next), (ahead, z_prev))):
                if 1 <= step <= 3 or (step == 4 and d == p):
                    got(slot(block, core, *cut), ring_sem(base, step - 1, d, p))
                if step < 3 or (step == 3 and d == p):
                    send(slot(block, core, *cut), slot(block, core, *cut), ring_sem(base, step, d, p), to)
        if step == 0 or step == 4:
            send(slot(back, core), slot(back, core), cbase + (7 if step else 0), twin)
        else:
            send(slot(back, core), slot(back, core), cbase + 2 * step - 1, twin)
            send(slot(ahead, core), slot(ahead, core), cbase + 2 * step, twin)

    def ring_order():
        return [(0, z)] + [
            (2 * s - 1 + d, (z + 8 - s) % 8 if d == 0 else (z + s) % 8) for s in (1, 2, 3) for d in (0, 1)
        ] + [(7, (z + 4) % 8)]

    def ring_sent(slot, base, cbase):
        for i in range(14):
            sent(slot(z, core, *pieces(slot)[0]), base + i)
        for i in range(8):
            sent(slot(z, core), cbase + i)

    def send_down(j):
        there = pl.ds(pl.multiple_of(oh * half + j * cw, cw), cw)
        send(wd_in.at[0, there], down_f.at[zh, chunk(j)], DN + j, partner)

    def send_saved(j):
        send(sg_in.at[0, :, cols(oh, j)], sg_f.at[zh, :, chunk(j)], SGX + j, partner)
        send(su_in.at[0, :, cols(oh, j)], su_f.at[zh, :, chunk(j)], SUX + j, partner)

    loads[1].wait()
    ring(dy_slot, DYR, DYC, 0)

    pl.loop(0, DN_FIRST)(send_down)

    loads[0].wait()
    x_slot_own = x_slot(z, core)
    x_slot_own[...] = x_stage[...].astype(F32).T.astype(BF)
    acc[...] = jnp.zeros_like(acc)

    for step in (1, 2, 3):
        ring(dy_slot, DYR, DYC, step)
        for x_step in X_BESIDE[step]:
            ring(x_slot, XR, XC, x_step)
    if DN_FIRST < NC:
        pl.loop(DN_FIRST, NC)(send_down)
    pl.loop(0, SG_FIRST)(send_saved)
    ring(dy_slot, DYR, DYC, 4)
    for x_step in X_BESIDE[4]:
        ring(x_slot, XR, XC, x_step)
    loads[2].wait()
    for i, zz in ring_order():
        got(dy_slot(zz, 1 - core), DYC + i)

    def partial_hidden(j):
        got(down_f.at[oh, chunk(j)], DN + j)

        @pl.loop(0, 4)
        def _(xx):
            rows = pl.ds(pl.multiple_of(xx * xb, xb), xb)
            hgs[j, xx] = (
                nt(dyf[0, rows, :], down_f[0, chunk(j), :]) + nt(dyf[1, rows, :], down_f[1, chunk(j), :])
            ).astype(BF)

        send(hgs.at[j, x1], rsr.at[j, 0], RS + 3 * j, x_next)
        send(hgs.at[j, x2], rsr.at[j, 1], RS + 3 * j + 1, x_far)
        send(hgs.at[j, x3], rsr.at[j, 2], RS + 3 * j + 2, x_prev)

    pl.loop(0, HG_FIRST)(partial_hidden)
    for x_step in X_AFTER:
        ring(x_slot, XR, XC, x_step)
    if SG_FIRST < NC:
        pl.loop(SG_FIRST, NC)(send_saved)
    for i in (3, 4, 5, 6):
        loads[i].wait()

    def send_weights(j):
        send(wg_in.at[0, :, cols(oh, j)], gate_f.at[zh, :, chunk(j)], GTX + j, partner)
        send(wu_in.at[0, :, cols(oh, j)], up_f.at[zh, :, chunk(j)], UPX + j, partner)

    def activations(j):
        for d in range(3):
            got(rsr.at[j, d], RS + 3 * j + d)
        got(sg_f.at[oh, :, chunk(j)], SGX + j)
        got(su_f.at[oh, :, chunk(j)], SUX + j)
        for part in range(2):
            rows = pl.ds(part * tb, tb)
            hidden_grad = hgs[j, x, rows, :].astype(F32)
            for d in range(3):
                hidden_grad = hidden_grad + rsr[j, d, rows, :].astype(F32)
            gate_pre = sg_f[part, :, chunk(j)].astype(F32)
            up_pre = su_f[part, :, chunk(j)].astype(F32)
            sigmoid_gate = jax.nn.sigmoid(gate_pre)
            silu_gate = gate_pre * sigmoid_gate
            slope = sigmoid_gate * (1.0 + gate_pre * (1.0 - sigmoid_gate))
            g[j, x, rows, :] = (hidden_grad * up_pre * slope).astype(BF)
            u[j, x, rows, :] = (hidden_grad * silu_gate).astype(BF)
            ht[j, x, :, rows] = (silu_gate * up_pre).T.astype(BF)
        for i, ref in enumerate((g, u)):
            send(ref.at[j, x], ref.at[j, x], AG + 4 * j + i, x_next)
            send(ref.at[j, x], ref.at[j, x], AG + 4 * j + 2 + i, x_prev)

    def send_hidden(j):
        send(ht.at[j, x], ht.at[j, x], HA + 2 * j, x_next)
        send(ht.at[j, x], ht.at[j, x], HA + 2 * j + 1, x_prev)

    def halves(ref, j, xx, second):
        size = ref.shape[2] // 2
        return ref.at[j, xx, pl.ds(second * size, size)]

    def pass_on(ref, j, base, far):
        got(ref.at[j, x3], base)
        send(halves(ref, j, x3, 0), halves(ref, j, x3, 0), far, x_next)

    def pass_back(ref, j, base, far):
        got(ref.at[j, x1], base)
        send(halves(ref, j, x1, 1), halves(ref, j, x1, 1), far, x_prev)

    def forward(j):
        for i, ref in enumerate((g, u)):
            pass_on(ref, j, AG + 4 * j + i, AF + 4 * j + i)
            pass_back(ref, j, AG + 4 * j + 2 + i, AF + 4 * j + 2 + i)

    def forward_hidden(j):
        pass_on(ht, j, HA + 2 * j, HF + 2 * j)
        pass_back(ht, j, HA + 2 * j + 1, HF + 2 * j + 1)

    def down_grad(j, at):
        total = nn(ht[j, 0], dyf[at, pl.ds(0, xb), :])
        for xx in range(1, 4):
            total = total + nn(ht[j, xx], dyf[at, pl.ds(xx * xb, xb), :])
        return total.astype(BF)

    def column_grad(j, at, ref):
        total = nn(xt[at, :, pl.ds(0, xb)], ref[j, 0])
        for xx in range(1, 4):
            total = total + nn(xt[at, :, pl.ds(xx * xb, xb)], ref[j, xx])
        return total.astype(BF)

    def keep(i, own, out, where, j):
        pltpu.make_async_copy(own.at[j], out.at[where], osem.at[j, i]).start()

    def column_grads(j):
        for i, ref in enumerate((g, u)):
            got(halves(ref, j, x2, 0), AF + 4 * j + i)
            got(halves(ref, j, x2, 1), AF + 4 * j + 2 + i)
        got(gate_f.at[oh, :, chunk(j)], GTX + j)
        got(up_f.at[oh, :, chunk(j)], UPX + j)

        @pl.loop(0, 4)
        def _(xx):
            rows = pl.ds(pl.multiple_of(xx * xb, xb), xb)
            for at in range(2):
                acc[at, rows, :] += nt(g[j, xx], gate_f[at, :, chunk(j)]) + nt(u[j, xx], up_f[at, :, chunk(j)])

        @pl.when(j == NC - 1)
        def _():
            for m in range(2):
                for at in range(2):
                    rows = pl.ds(pl.multiple_of((1 - core + 2 * m) * xb, xb), xb)
                    dxs[at, m] = acc[at, rows, :].astype(BF)
                    send(dxs.at[at, m], dxr.at[at, m], DXC + 2 * m + at, twin)

        for i, (ref, theirs, own, out) in enumerate(((g, wgs, owg, gg_out), (u, wus, owu, gu_out))):
            theirs[j] = column_grad(j, oh, ref)
            send(theirs.at[j], out.at[:, cols(zh, j)], WX + 3 * j + 1 + i, partner)

        for i, (ref, own, out) in enumerate(((g, owg, gg_out), (u, owu, gu_out))):
            own[j] = column_grad(j, zh, ref)
            keep(1 + i, own, out, (slice(None), cols(zh, j)), j)

    def row_grads(j):
        got(halves(ht, j, x2, 0), HF + 2 * j)
        got(halves(ht, j, x2, 1), HF + 2 * j + 1)
        wds[j] = down_grad(j, oh)
        send(wds.at[j], gd_out.at[cols(zh, j), :], WX + 3 * j, partner)
        owd[j] = down_grad(j, zh)
        keep(0, owd, gd_out, (cols(zh, j),), j)

    @pl.loop(0, NC + LAG)
    def _(i):
        @pl.when(i < NC)
        def _():
            activations(i)

        if HG_FIRST < NC:
            @pl.when(i < NC - HG_FIRST)
            def _():
                partial_hidden(i + HG_FIRST)

        for step, turn in X_TURNS:
            @pl.when(i == turn)
            def _():
                ring(x_slot, XR, XC, step)
                if step == 4:
                    for n, zz in ring_order():
                        got(x_slot(zz, 1 - core), XC + n)

        for turn, first in ((1, 0), (2, 2)):
            @pl.when(i == turn)
            def _():
                send_weights(first)
                send_weights(first + 1)

        @pl.when((i >= 1) & (i <= NC))
        def _():
            forward(i - 1)

        @pl.when(i == NC)
        def _():
            pl.loop(0, NC)(send_hidden)

        @pl.when(i >= LAG)
        def _():
            column_grads(i - LAG)

    pl.loop(0, NC)(forward_hidden)
    for m in range(2):
        for at in range(2):
            got(dxr.at[at, m], DXC + 2 * m + at)

    def part(zz, first=0, size=tb):
        at, late, m = zz // 4, (zz % 4) // 2, zz % 2
        mine = pl.ds(pl.multiple_of(((core + 2 * m) * 2 + late) * tb + first, 16), size)
        other = pl.ds(pl.multiple_of(late * tb + first, 16), size)
        return acc[at, mine, :] + dxr[at, m, other, :].astype(F32)

    ht2 = tb // 2

    def dx_sem(step, d, p):
        return DXR + 4 * step + 2 * d + p

    for step in range(4):
        for p in range(2):
            rows = pl.ds(p * ht2, ht2)
            for d in range(2):
                to = (z + 4 - step) % 8 if d == 0 else (z + 4 + step) % 8
                if step == 0 and p != d:
                    continue
                total = part(to, p * ht2, ht2)
                if step >= 2 or (step == 1 and p == d):
                    got(precv.at[d, step - 1, rows], dx_sem(step - 1, d, p))
                    total = total + precv[d, step - 1, rows, :].astype(F32)
                psend[d, step, rows, :] = total.astype(BF)
                send(psend.at[d, step, rows], precv.at[d, step, rows], dx_sem(step, d, p), z_next if d == 0 else z_prev)
        if step >= 1:
            row_grads(step - 1)

    for p in range(2):
        rows = pl.ds(p * ht2, ht2)
        total = part(z, p * ht2, ht2)
        for d in range(2):
            got(precv.at[d, 3, rows], dx_sem(3, d, p))
            total = total + precv[d, 3, rows, :].astype(F32)
        fin[rows, :] = total.astype(BF)
        send(fin.at[rows], prev_out.at[rows], FIN + p, y_prev)
    row_grads(NC - 1)
    for p in range(2):
        got(prev_out.at[pl.ds(p * ht2, ht2)], FIN + p)

    ring_sent(dy_slot, DYR, DYC)
    ring_sent(x_slot, XR, XC)

    @pl.loop(0, NC)
    def _(j):
        sent(down_f.at[0, chunk(j)], DN + j)
        for ref, base in ((sg_f, SGX), (su_f, SUX), (gate_f, GTX), (up_f, UPX)):
            sent(ref.at[0, :, chunk(j)], base + j)
        for d in range(3):
            sent(rsr.at[j, d], RS + 3 * j + d)
        for i, ref in enumerate((g, u)):
            for d in range(2):
                sent(ref.at[j, 0], AG + 4 * j + 2 * d + i)
                sent(halves(ref, j, 0, 0), AF + 4 * j + 2 * d + i)
        for d in range(2):
            sent(ht.at[j, 0], HA + 2 * j + d)
            sent(halves(ht, j, 0, 0), HF + 2 * j + d)
        mine = (gd_out.at[cols(zh, j), :], gg_out.at[:, cols(zh, j)], gu_out.at[:, cols(zh, j)])
        theirs = (gd_out.at[cols(oh, j), :], gg_out.at[:, cols(oh, j)], gu_out.at[:, cols(oh, j)])
        for i, (ref, own, out, arrived) in enumerate(zip((wds, wgs, wus), (owd, owg, owu), mine, theirs)):
            sent(ref.at[j], WX + 3 * j + i)
            pltpu.make_async_copy(own.at[j], out, osem.at[j, i]).wait()
            got(arrived, WX + 3 * j + i)

    for i in range(4):
        sent(dxs.at[0, 0], DXC + i)
    for step in range(4):
        for d in range(2):
            for p in range(2):
                if step > 0 or p == d:
                    sent(psend.at[d, step, pl.ds(0, ht2)], dx_sem(step, d, p))
    for p in range(2):
        sent(fin.at[pl.ds(0, ht2)], FIN + p)


def update(kick, w_ref, m_ref, n_ref, grad_ref, w_out, m_out):
    moved = (
        (1.0 - FRICTION) * m_ref[0]
        - kick * grad_ref[...].astype(F32)
        + (2.0 * FRICTION) ** 0.5 * n_ref[0].astype(F32)
    )
    m_out[0] = moved
    w_out[0] = (w_ref[0].astype(F32) + DRIFT * moved).astype(BF)


def update_all(kick, prev, gg, gu, gd, mg, mu, md, ng, nu, nd, wg, wu, wd, *outs):
    prev_out, wg_out, wu_out, wd_out, mg_out, mu_out, md_out = outs
    last = lax.axis_index("section") == lax.axis_size("section") - 1
    prev_out[0] = jnp.where(last, jnp.zeros_like(prev), prev[...])
    update(kick, wg, mg, ng, gg, wg_out, mg_out)
    update(kick, wu, mu, nu, gu, wu_out, mu_out)
    update(kick, wd, md, nd, gd, wd_out, md_out)


def shards(*args):
    x_in, sg_in = args[0], args[2]
    tb, fb = x_in.shape[1], x_in.shape[2]
    hb = sg_in.shape[2]
    half = hb // 2
    cw = half // NC
    tokens = tb * lax.axis_size("row")
    kick = float(tokens) ** (-0.5)
    v = pltpu.VMEM
    scratch = [
        v((tb, fb), BF),
        v((2, tokens, fb), BF),
        v((2, fb, tokens), BF),
        v((2, half, fb), BF),
        v((2, fb, half), BF),
        v((2, fb, half), BF),
        v((2, tb, half), BF),
        v((2, tb, half), BF),
        v((NC, 4, 2 * tb, cw), BF),
        v((NC, 3, 2 * tb, cw), BF),
        v((NC, 4, cw, 2 * tb), BF),
        v((NC, 4, 2 * tb, cw), BF),
        v((NC, 4, 2 * tb, cw), BF),
        v((NC, cw, fb), BF), v((NC, fb, cw), BF), v((NC, fb, cw), BF),
        v((NC, cw, fb), BF), v((NC, fb, cw), BF), v((NC, fb, cw), BF),
        v((2, tokens, fb), F32),
        v((2, 2, 2 * tb, fb), BF),
        v((2, 2, 2 * tb, fb), BF),
        v((2, 4, tb, fb), BF),
        v((2, 4, tb, fb), BF),
        v((tb, fb), BF),
        pltpu.SemaphoreType.DMA((NSEM,)),
        pltpu.SemaphoreType.DMA((NSEM,)),
        pltpu.SemaphoreType.DMA((7,)),
        pltpu.SemaphoreType.DMA((NC, 3)),
    ]
    shape = jax.ShapeDtypeStruct
    work = 12 * tokens * fb * hb
    prev, gg, gu, gd = pl.pallas_call(
        kernel,
        out_shape=(shape((tb, fb), BF), shape((fb, hb), BF), shape((fb, hb), BF), shape((hb, fb), BF)),
        in_specs=[pl.BlockSpec(memory_space=pltpu.HBM)] * 7,
        out_specs=[pl.BlockSpec(memory_space=pl.ANY)] * 4,
        scratch_shapes=scratch,
        compiler_params=pltpu.CompilerParams(
            collective_id=1, has_side_effects=True, vmem_limit_bytes=52 << 20
        ),
        cost_estimate=pl.CostEstimate(flops=work, bytes_accessed=12 << 20, transcendentals=0),
        name="relayed_gradients",
    )(*args[:7])

    steps = 4
    thin, wide = pl.BlockSpec((fb // steps, hb), lambda i: (i, 0)), pl.BlockSpec((1, fb // steps, hb), lambda i: (0, i, 0))
    low, tall = pl.BlockSpec((hb // steps, fb), lambda i: (i, 0)), pl.BlockSpec((1, hb // steps, fb), lambda i: (0, i, 0))
    block, block_out = pl.BlockSpec((tb // steps, fb), lambda i: (i, 0)), pl.BlockSpec((1, tb // steps, fb), lambda i: (0, i, 0))
    outs = (
        shape(args[0].shape, BF),
        shape(args[4].shape, BF), shape(args[5].shape, BF), shape(args[6].shape, BF),
        shape(args[7].shape, F32), shape(args[8].shape, F32), shape(args[9].shape, F32),
    )
    return pl.pallas_call(
        functools.partial(update_all, kick),
        grid=(steps,),
        out_shape=outs,
        in_specs=[block, thin, thin, low] + [wide, wide, tall] * 3,
        out_specs=[block_out] + [wide, wide, tall] * 2,
        compiler_params=pltpu.CompilerParams(vmem_limit_bytes=16 << 20),
        name="sghmc_update",
    )(prev, gg, gu, gd, *args[7:10], *args[10:13], *args[4:7])


def solution(mesh):
    feature = P("section", "col", "row")
    hidden = P("section", "row", "col")
    in_specs = (
        feature, feature, hidden, hidden, hidden, hidden, feature,
        hidden, hidden, feature, hidden, hidden, feature,
    )
    out_specs = (feature, hidden, hidden, feature, hidden, hidden, feature)
    return jax.shard_map(shards, mesh=mesh, in_specs=in_specs, out_specs=out_specs, check_vma=False)
```

```python
import functools

import jax
import jax.numpy as jnp
from jax import lax
from jax.experimental import pallas as pl
from jax.experimental.pallas import tpu as pltpu
from jax.sharding import PartitionSpec as P

FRICTION = 0.1
DRIFT = 0.01
MESH = pl.DeviceIdType.MESH
BF = jnp.bfloat16
F32 = jnp.float32
NC = 4
DN_FIRST = 4
SG_FIRST = 2
HG_FIRST = 2
X_FIRST = True
X_BESIDE = {1: (), 2: (), 3: (0,), 4: ()}
LAG = 3
X_AFTER = ()
X_TURNS = ((1, 0), (2, 1), (3, 2), (4, 3))

DN, SGX, SUX, GTX, UPX = 0, NC, 2 * NC, 3 * NC, 4 * NC
DYR = 5 * NC
DYC = DYR + 14
XR = DYC + 8
XC = XR + 14
RS = XC + 8
AG = RS + 3 * NC
AF = AG + 4 * NC
WX = AF + 4 * NC
HA = WX + 3 * NC
HF = HA + 2 * NC
DXC = HF + 2 * NC
DXR = DXC + 4
FIN = DXR + 16
HE = FIN + 2
NSEM = HE + 4


def nt(a, b):
    return lax.dot_general(a, b, (((1,), (1,)), ((), ())), preferred_element_type=F32)


def nn(a, b):
    return jnp.dot(a, b, preferred_element_type=F32)


def kernel(
    x_in, dy_in, sg_in, su_in, wg_in, wu_in, wd_in,
    prev_out, gg_out, gu_out, gd_out,
    x_stage, dyf, xt, down_f, gate_f, up_f, sg_f, su_f, hgs, rsr, ht, g, u,
    wds, wgs, wus, owd, owg, owu, acc, dxs, dxr, psend, precv, fin,
    ssem, rsem, lsem, osem,
):
    tb, fb = x_in.shape[1], x_in.shape[2]
    half = sg_in.shape[2] // 2
    cw = half // NC
    xb = 2 * tb

    y, row, col = lax.axis_index("section"), lax.axis_index("row"), lax.axis_index("col")
    zh, x, zl, core = row // 4, row % 4, col // 2, col % 2
    z = zh * 4 + zl
    oh = 1 - zh

    def at_z(zz):
        return (y, (zz // 4) * 4 + x, (zz % 4) * 2 + core)

    def at_x(xx):
        return (y, zh * 4 + xx, col)

    partner = (y, oh * 4 + x, col)
    z_next, z_prev = at_z((z + 1) % 8), at_z((z + 7) % 8)
    x1, x2, x3 = (x + 1) % 4, (x + 2) % 4, (x + 3) % 4
    x_next, x_prev, x_far = at_x(x1), at_x(x3), at_x(x2)
    twin = (y, row, zl * 2 + 1 - core)
    y_prev, y_next = ((y + 3) % 4, row, col), ((y + 1) % 4, row, col)

    def rcopy(src, dst, sem, to):
        return pltpu.make_async_remote_copy(
            src_ref=src, dst_ref=dst, send_sem=ssem.at[sem], recv_sem=rsem.at[sem],
            device_id=to, device_id_type=MESH,
        )

    def send(src, dst, sem, to):
        rcopy(src, dst, sem, to).start()

    def got(dst, sem):
        rcopy(dst, dst, sem, partner).wait_recv()

    def sent(src, sem):
        rcopy(src, src, sem, partner).wait_send()

    def cols(at, j):
        return pl.ds(pl.multiple_of(at * half + j * cw, cw), cw)

    def chunk(j):
        return pl.ds(pl.multiple_of(j * cw, cw), cw)

    def place(zz, kk):
        return ((((zz % 2) * 2 + kk) * 2) + (zz % 4) // 2) * tb

    def dy_slot(zz, kk, first=0, size=tb):
        return dyf.at[zz // 4, pl.ds(pl.multiple_of(place(zz, kk) + first, 16), size)]

    def x_slot(zz, kk, first=0, size=fb):
        return xt.at[zz // 4, pl.ds(first, size), pl.ds(pl.multiple_of(place(zz, kk), tb), tb)]

    bar = pltpu.get_barrier_semaphore()
    for to in (partner, z_next, z_prev, x_next, x_prev, x_far, twin, y_next):
        pl.semaphore_signal(bar, inc=1, device_id=to, device_id_type=MESH)

    own_half = pl.ds(pl.multiple_of(zh * half, half), half)
    loads = [
        pltpu.make_async_copy(s, d, lsem.at[i])
        for i, (s, d) in enumerate([
            (x_in.at[0], x_stage),
            (dy_in.at[0], dy_slot(z, core)),
            (wd_in.at[0, own_half], down_f.at[zh]),
            (sg_in.at[0, :, own_half], sg_f.at[zh]),
            (su_in.at[0, :, own_half], su_f.at[zh]),
            (wg_in.at[0, :, own_half], gate_f.at[zh]),
            (wu_in.at[0, :, own_half], up_f.at[zh]),
        ])
    ]
    for load in loads:
        load.start()
    pl.semaphore_wait(bar, 8)

    def pieces(slot):
        size = (tb if slot is dy_slot else fb) // 2
        return (0, size), (size, size)

    def ring_sem(base, step, d, p):
        return base + (4 * step + 2 * d + p if step < 3 else 12 + d)

    def ring(slot, base, cbase, step):
        back, ahead = (z + 8 - step) % 8, (z + step) % 8
        for p, cut in enumerate(pieces(slot)):
            for d, (block, to) in enumerate(((back, z_next), (ahead, z_prev))):
                if 1 <= step <= 3 or (step == 4 and d == p):
                    got(slot(block, core, *cut), ring_sem(base, step - 1, d, p))
                if step < 3 or (step == 3 and d == p):
                    send(slot(block, core, *cut), slot(block, core, *cut), ring_sem(base, step, d, p), to)
        if step == 0 or step == 4:
            send(slot(back, core), slot(back, core), cbase + (7 if step else 0), twin)
        else:
            send(slot(back, core), slot(back, core), cbase + 2 * step - 1, twin)
            send(slot(ahead, core), slot(ahead, core), cbase + 2 * step, twin)

    def ring_order():
        return [(0, z)] + [
            (2 * s - 1 + d, (z + 8 - s) % 8 if d == 0 else (z + s) % 8) for s in (1, 2, 3) for d in (0, 1)
        ] + [(7, (z + 4) % 8)]

    def ring_sent(slot, base, cbase):
        for i in range(14):
            sent(slot(z, core, *pieces(slot)[0]), base + i)
        for i in range(8):
            sent(slot(z, core), cbase + i)

    def send_down(j):
        there = pl.ds(pl.multiple_of(oh * half + j * cw, cw), cw)
        send(wd_in.at[0, there], down_f.at[zh, chunk(j)], DN + j, partner)

    def send_saved(j):
        send(sg_in.at[0, :, cols(oh, j)], sg_f.at[zh, :, chunk(j)], SGX + j, partner)
        send(su_in.at[0, :, cols(oh, j)], su_f.at[zh, :, chunk(j)], SUX + j, partner)

    loads[1].wait()
    ring(dy_slot, DYR, DYC, 0)

    pl.loop(0, DN_FIRST)(send_down)

    loads[0].wait()
    x_slot_own = x_slot(z, core)
    x_slot_own[...] = x_stage[...].astype(F32).T.astype(BF)

    def token_columns(part):
        return pl.ds(pl.multiple_of(part * tb, tb), tb)

    def cut_rows(second):
        return pl.ds(0, cw) if second is None else pl.ds(second * (cw // 2), cw // 2)

    def early(xx, second=None):
        return ht.at[:, xx, cut_rows(second), token_columns(zh)]

    def late(j, xx, second=None):
        return ht.at[j, xx, cut_rows(second), token_columns(oh)]

    def hidden_value(part, j):
        gate_pre = sg_f[part, :, chunk(j)].astype(F32)
        up_pre = su_f[part, :, chunk(j)].astype(F32)
        value = gate_pre * jax.nn.sigmoid(gate_pre) * up_pre
        ht[j, x, :, token_columns(part)] = value.T.astype(BF)

    loads[3].wait()
    loads[4].wait()
    pl.loop(0, NC)(functools.partial(hidden_value, zh))
    send(early(x), early(x), HE, x_next)
    send(early(x), early(x), HE + 1, x_prev)
    acc[...] = jnp.zeros_like(acc)

    for step in (1, 2, 3):
        ring(dy_slot, DYR, DYC, step)
        for x_step in X_BESIDE[step]:
            ring(x_slot, XR, XC, x_step)
    if DN_FIRST < NC:
        pl.loop(DN_FIRST, NC)(send_down)
    pl.loop(0, SG_FIRST)(send_saved)
    ring(dy_slot, DYR, DYC, 4)
    got(early(x3), HE)
    send(early(x3, 0), early(x3, 0), HE + 2, x_next)
    got(early(x1), HE + 1)
    send(early(x1, 1), early(x1, 1), HE + 3, x_prev)
    for x_step in X_BESIDE[4]:
        ring(x_slot, XR, XC, x_step)
    loads[2].wait()
    for i, zz in ring_order():
        got(dy_slot(zz, 1 - core), DYC + i)

    def partial_hidden(j):
        got(down_f.at[oh, chunk(j)], DN + j)

        @pl.loop(0, 4)
        def _(xx):
            rows = pl.ds(pl.multiple_of(xx * xb, xb), xb)
            hgs[j, xx] = (
                nt(dyf[0, rows, :], down_f[0, chunk(j), :]) + nt(dyf[1, rows, :], down_f[1, chunk(j), :])
            ).astype(BF)

        send(hgs.at[j, x1], rsr.at[j, 0], RS + 3 * j, x_next)
        send(hgs.at[j, x2], rsr.at[j, 1], RS + 3 * j + 1, x_far)
        send(hgs.at[j, x3], rsr.at[j, 2], RS + 3 * j + 2, x_prev)

    pl.loop(0, HG_FIRST)(partial_hidden)
    for x_step in X_AFTER:
        ring(x_slot, XR, XC, x_step)
    if SG_FIRST < NC:
        pl.loop(SG_FIRST, NC)(send_saved)
    for i in (5, 6):
        loads[i].wait()

    def send_weights(j):
        send(wg_in.at[0, :, cols(oh, j)], gate_f.at[zh, :, chunk(j)], GTX + j, partner)
        send(wu_in.at[0, :, cols(oh, j)], up_f.at[zh, :, chunk(j)], UPX + j, partner)

    def activations(j):
        for d in range(3):
            got(rsr.at[j, d], RS + 3 * j + d)
        got(sg_f.at[oh, :, chunk(j)], SGX + j)
        got(su_f.at[oh, :, chunk(j)], SUX + j)
        hidden_value(oh, j)
        for part in range(2):
            rows = pl.ds(part * tb, tb)
            hidden_grad = hgs[j, x, rows, :].astype(F32)
            for d in range(3):
                hidden_grad = hidden_grad + rsr[j, d, rows, :].astype(F32)
            gate_pre = sg_f[part, :, chunk(j)].astype(F32)
            up_pre = su_f[part, :, chunk(j)].astype(F32)
            sigmoid_gate = jax.nn.sigmoid(gate_pre)
            slope = sigmoid_gate * (1.0 + gate_pre * (1.0 - sigmoid_gate))
            g[j, x, rows, :] = (hidden_grad * up_pre * slope).astype(BF)
            u[j, x, rows, :] = (hidden_grad * (gate_pre * sigmoid_gate)).astype(BF)
        for i, ref in enumerate((g, u)):
            send(ref.at[j, x], ref.at[j, x], AG + 4 * j + i, x_next)
            send(ref.at[j, x], ref.at[j, x], AG + 4 * j + 2 + i, x_prev)

    def send_hidden(j):
        send(late(j, x), late(j, x), HA + 2 * j, x_next)
        send(late(j, x), late(j, x), HA + 2 * j + 1, x_prev)

    def halves(ref, j, xx, second):
        size = ref.shape[2] // 2
        return ref.at[j, xx, pl.ds(second * size, size)]

    def pass_on(ref, j, base, far):
        got(ref.at[j, x3], base)
        send(halves(ref, j, x3, 0), halves(ref, j, x3, 0), far, x_next)

    def pass_back(ref, j, base, far):
        got(ref.at[j, x1], base)
        send(halves(ref, j, x1, 1), halves(ref, j, x1, 1), far, x_prev)

    def forward(j):
        for i, ref in enumerate((g, u)):
            pass_on(ref, j, AG + 4 * j + i, AF + 4 * j + i)
            pass_back(ref, j, AG + 4 * j + 2 + i, AF + 4 * j + 2 + i)

    def forward_hidden(j):
        got(late(j, x3), HA + 2 * j)
        send(late(j, x3, 0), late(j, x3, 0), HF + 2 * j, x_next)
        got(late(j, x1), HA + 2 * j + 1)
        send(late(j, x1, 1), late(j, x1, 1), HF + 2 * j + 1, x_prev)

    def down_grad(j, at):
        total = nn(ht[j, 0], dyf[at, pl.ds(0, xb), :])
        for xx in range(1, 4):
            total = total + nn(ht[j, xx], dyf[at, pl.ds(xx * xb, xb), :])
        return total.astype(BF)

    def column_grad(j, at, ref):
        total = nn(xt[at, :, pl.ds(0, xb)], ref[j, 0])
        for xx in range(1, 4):
            total = total + nn(xt[at, :, pl.ds(xx * xb, xb)], ref[j, xx])
        return total.astype(BF)

    def keep(i, own, out, where, j):
        pltpu.make_async_copy(own.at[j], out.at[where], osem.at[j, i]).start()

    def partner_columns(j):
        for i, ref in enumerate((g, u)):
            got(halves(ref, j, x2, 0), AF + 4 * j + i)
            got(halves(ref, j, x2, 1), AF + 4 * j + 2 + i)
        send_columns(j)

    def send_columns(j):
        for i, (ref, theirs, out) in enumerate(((g, wgs, gg_out), (u, wus, gu_out))):
            theirs[j] = column_grad(j, oh, ref)
            send(theirs.at[j], out.at[:, cols(zh, j)], WX + 3 * j + 1 + i, partner)

    def own_columns(j):
        for i, (ref, own, out) in enumerate(((g, owg, gg_out), (u, owu, gu_out))):
            own[j] = column_grad(j, zh, ref)
            keep(1 + i, own, out, (slice(None), cols(zh, j)), j)

    def add_input_grad(j):
        got(gate_f.at[oh, :, chunk(j)], GTX + j)
        got(up_f.at[oh, :, chunk(j)], UPX + j)

        @pl.loop(0, 4)
        def _(xx):
            rows = pl.ds(pl.multiple_of(xx * xb, xb), xb)
            for at in range(2):
                acc[at, rows, :] += nt(g[j, xx], gate_f[at, :, chunk(j)]) + nt(u[j, xx], up_f[at, :, chunk(j)])

    def row_grads(j):
        got(late(j, x2, 0), HF + 2 * j)
        got(late(j, x2, 1), HF + 2 * j + 1)
        wds[j] = down_grad(j, oh)
        send(wds.at[j], gd_out.at[cols(zh, j), :], WX + 3 * j, partner)
        owd[j] = down_grad(j, zh)
        keep(0, owd, gd_out, (cols(zh, j),), j)

    @pl.loop(0, NC + 1)
    def _(i):
        @pl.when(i < NC)
        def _():
            activations(i)

        if HG_FIRST < NC:
            @pl.when(i < NC - HG_FIRST)
            def _():
                partial_hidden(i + HG_FIRST)

        for step, turn in X_TURNS:
            @pl.when(i == turn)
            def _():
                ring(x_slot, XR, XC, step)
                if step == 4:
                    for n, zz in ring_order():
                        got(x_slot(zz, 1 - core), XC + n)

        for turn, first in ((1, 0), (2, 2)):
            @pl.when(i == turn)
            def _():
                send_weights(first)
                send_weights(first + 1)

        @pl.when((i >= 1) & (i <= NC))
        def _():
            forward(i - 1)

        @pl.when(i == NC)
        def _():
            pl.loop(0, NC)(send_hidden)

        @pl.when((i == NC - 1) | (i == NC))
        def _():
            pl.loop(jnp.where(i == NC, 1, 0), jnp.where(i == NC, NC - 1, 1))(partner_columns)

        @pl.when(i == NC)
        def _():
            pl.loop(0, NC - 1)(add_input_grad)

    for i, ref in enumerate((g, u)):
        got(halves(ref, NC - 1, x2, 0), AF + 4 * (NC - 1) + i)
        got(halves(ref, NC - 1, x2, 1), AF + 4 * (NC - 1) + 2 + i)
    add_input_grad(NC - 1)
    for m in range(2):
        for at in range(2):
            rows = pl.ds(pl.multiple_of((1 - core + 2 * m) * xb, xb), xb)
            dxs[at, m] = acc[at, rows, :].astype(BF)
            send(dxs.at[at, m], dxr.at[at, m], DXC + 2 * m + at, twin)
    send_columns(NC - 1)

    pl.loop(0, NC)(forward_hidden)
    got(early(x2, 0), HE + 2)
    got(early(x2, 1), HE + 3)
    for m in range(2):
        for at in range(2):
            got(dxr.at[at, m], DXC + 2 * m + at)

    def part(zz, first=0, size=tb):
        at, late, m = zz // 4, (zz % 4) // 2, zz % 2
        mine = pl.ds(pl.multiple_of(((core + 2 * m) * 2 + late) * tb + first, 16), size)
        other = pl.ds(pl.multiple_of(late * tb + first, 16), size)
        return acc[at, mine, :] + dxr[at, m, other, :].astype(F32)

    ht2 = tb // 2

    def dx_sem(step, d, p):
        return DXR + 4 * step + 2 * d + p

    for step in range(4):
        for p in range(2):
            rows = pl.ds(p * ht2, ht2)
            for d in range(2):
                to = (z + 4 - step) % 8 if d == 0 else (z + 4 + step) % 8
                if step == 0 and p != d:
                    continue
                total = part(to, p * ht2, ht2)
                if step >= 2 or (step == 1 and p == d):
                    got(precv.at[d, step - 1, rows], dx_sem(step - 1, d, p))
                    total = total + precv[d, step - 1, rows, :].astype(F32)
                psend[d, step, rows, :] = total.astype(BF)
                send(psend.at[d, step, rows], precv.at[d, step, rows], dx_sem(step, d, p), z_next if d == 0 else z_prev)
        if step >= 1:
            own_columns(step - 1)
            row_grads(step - 1)

    for p in range(2):
        rows = pl.ds(p * ht2, ht2)
        total = part(z, p * ht2, ht2)
        for d in range(2):
            got(precv.at[d, 3, rows], dx_sem(3, d, p))
            total = total + precv[d, 3, rows, :].astype(F32)
        fin[rows, :] = total.astype(BF)
        send(fin.at[rows], prev_out.at[rows], FIN + p, y_prev)
    own_columns(NC - 1)
    row_grads(NC - 1)
    for p in range(2):
        got(prev_out.at[pl.ds(p * ht2, ht2)], FIN + p)

    ring_sent(dy_slot, DYR, DYC)
    ring_sent(x_slot, XR, XC)

    @pl.loop(0, NC)
    def _(j):
        sent(down_f.at[0, chunk(j)], DN + j)
        for ref, base in ((sg_f, SGX), (su_f, SUX), (gate_f, GTX), (up_f, UPX)):
            sent(ref.at[0, :, chunk(j)], base + j)
        for d in range(3):
            sent(rsr.at[j, d], RS + 3 * j + d)
        for i, ref in enumerate((g, u)):
            for d in range(2):
                sent(ref.at[j, 0], AG + 4 * j + 2 * d + i)
                sent(halves(ref, j, 0, 0), AF + 4 * j + 2 * d + i)
        for d in range(2):
            sent(late(j, 0), HA + 2 * j + d)
            sent(late(j, 0, 0), HF + 2 * j + d)
        mine = (gd_out.at[cols(zh, j), :], gg_out.at[:, cols(zh, j)], gu_out.at[:, cols(zh, j)])
        theirs = (gd_out.at[cols(oh, j), :], gg_out.at[:, cols(oh, j)], gu_out.at[:, cols(oh, j)])
        for i, (ref, own, out, arrived) in enumerate(zip((wds, wgs, wus), (owd, owg, owu), mine, theirs)):
            sent(ref.at[j], WX + 3 * j + i)
            pltpu.make_async_copy(own.at[j], out, osem.at[j, i]).wait()
            got(arrived, WX + 3 * j + i)

    for d in range(2):
        sent(early(0), HE + d)
        sent(early(0, 0), HE + 2 + d)
    for i in range(4):
        sent(dxs.at[0, 0], DXC + i)
    for step in range(4):
        for d in range(2):
            for p in range(2):
                if step > 0 or p == d:
                    sent(psend.at[d, step, pl.ds(0, ht2)], dx_sem(step, d, p))
    for p in range(2):
        sent(fin.at[pl.ds(0, ht2)], FIN + p)


def update(kick, w_ref, m_ref, n_ref, grad_ref, w_out, m_out):
    moved = (
        (1.0 - FRICTION) * m_ref[0]
        - kick * grad_ref[...].astype(F32)
        + (2.0 * FRICTION) ** 0.5 * n_ref[0].astype(F32)
    )
    m_out[0] = moved
    w_out[0] = (w_ref[0].astype(F32) + DRIFT * moved).astype(BF)


def update_all(kick, prev, gg, gu, gd, mg, mu, md, ng, nu, nd, wg, wu, wd, *outs):
    prev_out, wg_out, wu_out, wd_out, mg_out, mu_out, md_out = outs
    last = lax.axis_index("section") == lax.axis_size("section") - 1
    prev_out[0] = jnp.where(last, jnp.zeros_like(prev), prev[...])
    update(kick, wg, mg, ng, gg, wg_out, mg_out)
    update(kick, wu, mu, nu, gu, wu_out, mu_out)
    update(kick, wd, md, nd, gd, wd_out, md_out)


def shards(*args):
    x_in, sg_in = args[0], args[2]
    tb, fb = x_in.shape[1], x_in.shape[2]
    hb = sg_in.shape[2]
    half = hb // 2
    cw = half // NC
    tokens = tb * lax.axis_size("row")
    kick = float(tokens) ** (-0.5)
    v = pltpu.VMEM
    scratch = [
        v((tb, fb), BF),
        v((2, tokens, fb), BF),
        v((2, fb, tokens), BF),
        v((2, half, fb), BF),
        v((2, fb, half), BF),
        v((2, fb, half), BF),
        v((2, tb, half), BF),
        v((2, tb, half), BF),
        v((NC, 4, 2 * tb, cw), BF),
        v((NC, 3, 2 * tb, cw), BF),
        v((NC, 4, cw, 2 * tb), BF),
        v((NC, 4, 2 * tb, cw), BF),
        v((NC, 4, 2 * tb, cw), BF),
        v((NC, cw, fb), BF), v((NC, fb, cw), BF), v((NC, fb, cw), BF),
        v((NC, cw, fb), BF), v((NC, fb, cw), BF), v((NC, fb, cw), BF),
        v((2, tokens, fb), F32),
        v((2, 2, 2 * tb, fb), BF),
        v((2, 2, 2 * tb, fb), BF),
        v((2, 4, tb, fb), BF),
        v((2, 4, tb, fb), BF),
        v((tb, fb), BF),
        pltpu.SemaphoreType.DMA((NSEM,)),
        pltpu.SemaphoreType.DMA((NSEM,)),
        pltpu.SemaphoreType.DMA((7,)),
        pltpu.SemaphoreType.DMA((NC, 3)),
    ]
    shape = jax.ShapeDtypeStruct
    work = 12 * tokens * fb * hb
    prev, gg, gu, gd = pl.pallas_call(
        kernel,
        out_shape=(shape((tb, fb), BF), shape((fb, hb), BF), shape((fb, hb), BF), shape((hb, fb), BF)),
        in_specs=[pl.BlockSpec(memory_space=pltpu.HBM)] * 7,
        out_specs=[pl.BlockSpec(memory_space=pl.ANY)] * 4,
        scratch_shapes=scratch,
        compiler_params=pltpu.CompilerParams(
            collective_id=1, has_side_effects=True, vmem_limit_bytes=52 << 20
        ),
        cost_estimate=pl.CostEstimate(flops=work, bytes_accessed=12 << 20, transcendentals=0),
        name="relayed_gradients",
    )(*args[:7])

    steps = 4
    thin, wide = pl.BlockSpec((fb // steps, hb), lambda i: (i, 0)), pl.BlockSpec((1, fb // steps, hb), lambda i: (0, i, 0))
    low, tall = pl.BlockSpec((hb // steps, fb), lambda i: (i, 0)), pl.BlockSpec((1, hb // steps, fb), lambda i: (0, i, 0))
    block, block_out = pl.BlockSpec((tb // steps, fb), lambda i: (i, 0)), pl.BlockSpec((1, tb // steps, fb), lambda i: (0, i, 0))
    outs = (
        shape(args[0].shape, BF),
        shape(args[4].shape, BF), shape(args[5].shape, BF), shape(args[6].shape, BF),
        shape(args[7].shape, F32), shape(args[8].shape, F32), shape(args[9].shape, F32),
    )
    return pl.pallas_call(
        functools.partial(update_all, kick),
        grid=(steps,),
        out_shape=outs,
        in_specs=[block, thin, thin, low] + [wide, wide, tall] * 3,
        out_specs=[block_out] + [wide, wide, tall] * 2,
        compiler_params=pltpu.CompilerParams(vmem_limit_bytes=16 << 20),
        name="sghmc_update",
    )(prev, gg, gu, gd, *args[7:10], *args[10:13], *args[4:7])


def solution(mesh):
    feature = P("section", "col", "row")
    hidden = P("section", "row", "col")
    in_specs = (
        feature, feature, hidden, hidden, hidden, hidden, feature,
        hidden, hidden, feature, hidden, hidden, feature,
    )
    out_specs = (feature, hidden, hidden, feature, hidden, hidden, feature)
    return jax.shard_map(shards, mesh=mesh, in_specs=in_specs, out_specs=out_specs, check_vma=False)
```
